32 devices in a mesh: sample: 8 (over z, y), variant: 4 (over x, core).
Axes of the slice: x: 2, y: 2, z: 4, core: 2. Of those that a mesh axis runs over, the one named last changes fastest.
Arguments:
- dosage: bfloat16 [4096, 2048], P('sample', 'variant'), may hold values from 0 to 2
- covariates: float32 [30, 4096], P(None, 'sample'), may hold values from -6 to 6
- reach: int32 [4], replicated, may hold values from 1 to 2, as said below
Outputs:
- ld_bands: bfloat16 [4, 2048, 512], P(None, ('variant', 'sample'))
The draws below stay inside these ranges and needn't reach their ends.
Inputs may be any that keep to these rules, and one draw needn't show every extreme that they name: `reach`: every draw has a block whose band reaches 2 blocks on each side.
All inputs are finite; a program needn't handle non-finite values.
Results may differ from the reference program's by a relative error of at most 0.015.
Values may be sent and summed in bfloat16 or wider, within the bound.
A program may use at most 64 MiB of HBM per device.

```python
import math
import jax
import jax.numpy as jnp
from jax import lax

VB = 512
K = 30
MAXR = 2
S = 4096
NB = 4
V = 2048


def shared_covariates(key):
    values = jax.random.normal(jax.random.fold_in(key, 11), (K, S), jnp.float32)
    return jnp.clip(values, -6.0, 6.0)


def draw_covariates(key, part):
    return shared_covariates(key)


def draw_dosage(key, part):
    values = shared_covariates(key)
    loading = jax.random.normal(jax.random.fold_in(key, 13), (K, V), jnp.float32) / jnp.sqrt(float(K))
    noise = jax.random.uniform(jax.random.fold_in(key, 14), (S, V), jnp.float32, -1.0, 1.0)
    linked = jnp.dot(values.T, loading)
    return jnp.clip(1.0 + 0.3 * linked + 0.45 * noise, 0.0, 2.0).astype(jnp.bfloat16)


def draw_reach(key, part):
    base = jax.random.randint(jax.random.fold_in(key, 21), (NB,), 1, MAXR + 1)
    chosen = jax.random.randint(jax.random.fold_in(key, 22), (), 0, NB)
    return jnp.where(jnp.arange(NB) == chosen, MAXR, base).astype(jnp.int32)


def setup_inputs(seed: int = 0) -> dict:
    streams_of = jax.random.split(jax.random.key(seed), 4)
    return {
        "dosage": draw_dosage(jax.random.fold_in(streams_of[3], 71), 0),
        "covariates": draw_covariates(jax.random.fold_in(streams_of[3], 71), 0),
        "reach": draw_reach(jax.random.fold_in(streams_of[3], 71), 0),
    }


def reference(dosage, covariates, reach):
    highest = lax.Precision.HIGHEST
    samples = dosage.shape[0]
    blocks_count = reach.shape[0]
    design = jnp.concatenate([jnp.ones((1, samples), jnp.float32), covariates.astype(jnp.float32)], 0)
    genotype = dosage.astype(jnp.float32)
    moment = jnp.dot(design, design.T, precision=highest)
    cross = jnp.dot(design, genotype, precision=highest)
    factor = jnp.linalg.cholesky(moment)
    coefficients = jax.scipy.linalg.cho_solve((factor, True), cross)
    residual = genotype - jnp.dot(design.T, coefficients, precision=highest)
    spread = lax.optimization_barrier(jnp.sum(residual * residual, 0))
    scaled = (residual * jnp.sqrt(samples / spread)).astype(jnp.bfloat16)
    stacked = scaled.reshape(samples, blocks_count, VB).transpose(1, 0, 2)
    inverse_root = 1.0 / math.sqrt(samples)

    def one_block(index):
        left = stacked[index].astype(jnp.float32)
        tiles = []
        for slot in range(2 * MAXR):
            offset = slot - MAXR if slot < MAXR else slot - MAXR + 1
            other = ((index + offset) % blocks_count).astype(jnp.int32)
            right = stacked[other].astype(jnp.float32)
            tile = lax.dot_general(left, right, (((0,), (0,)), ((), ())), precision=highest) * inverse_root
            live = abs(offset) <= reach[index]
            tiles.append(jnp.where(live, tile, 0.0).astype(jnp.bfloat16))
        return jnp.stack(tiles)
    result = lax.map(one_block, jnp.arange(blocks_count, dtype=jnp.int32))
    return result.transpose(1, 0, 2, 3).reshape(2 * MAXR, blocks_count * VB, VB)
```

```python
import functools
import math

import jax
import jax.numpy as jnp
from jax import lax
from jax.experimental import pallas as pl
from jax.experimental.pallas import tpu as pltpu
from jax.sharding import PartitionSpec as P

MAXR = 2
ROWS = 8
LANES = 128
MESH = pl.DeviceIdType.MESH
HIGHEST = lax.Precision.HIGHEST
F32 = jnp.float32
BF16 = jnp.bfloat16


def exact_dot(a, b, dims):
    return lax.dot_general(a, b, (dims, ((), ())), precision=HIGHEST, preferred_element_type=F32)


def fast_dot(a, b, dims):
    return lax.dot_general(a, b, (dims, ((), ())), preferred_element_type=F32)


def inverse(matrix):
    size = matrix.shape[0]
    row_at = lax.broadcasted_iota(jnp.int32, matrix.shape, 0)
    lane_at = lax.broadcasted_iota(jnp.int32, matrix.shape, 1)

    def step(k, a):
        row = jnp.sum(jnp.where(row_at == k, a, 0.0), 0, keepdims=True)
        column = jnp.sum(jnp.where(lane_at == k, a, 0.0), 1, keepdims=True)
        pivot = jnp.sum(jnp.where(lane_at[:1] == k, row, 0.0), 1, keepdims=True)
        row = jnp.where(lane_at[:1] == k, 1.0, row) / pivot
        rest = jnp.where(lane_at == k, 0.0, a) - column * row
        return jnp.where(row_at == k, row, rest)

    return lax.fori_loop(0, size, step, matrix)


def kernel(
    ns, nb, dosage, covariates, out,
    design, cross, cross_out, cross_in, cross_sum, moments, coefs, blocks, own_t, others,
    spreads, tiles, pair_out, pair_in, ring_out, ring_in, turn_out, turn_in, back_out, back_in,
    block_send, block_recv, cross_send, cross_recv, moment_send, moment_recv, sum_send, sum_recv,
    coef_send, coef_recv, spread_send, spread_recv, pair_send, pair_recv, ring_send, ring_recv,
    turn_send, turn_recv, back_send, back_recv,
):
    s = lax.axis_index("sample")
    v = lax.axis_index("variant")
    local, width = dosage.shape
    terms = covariates.shape[0] + 1
    depth = cross.shape[0]
    across = ns // (depth // ROWS)
    piece = width // across
    groups = ns // 2
    group, half = lax.div(s, 2), lax.rem(s, 2)
    rows = width // ns

    def sample_peer(j):
        return lax.rem(s + j, ns)

    def variant_peer(j):
        return lax.rem(v + j + nb, nb)

    def copy(src, dst, send, recv, sample, variant):
        return pltpu.make_async_remote_copy(
            src_ref=src, dst_ref=dst, send_sem=send, recv_sem=recv,
            device_id=(sample, variant), device_id_type=MESH,
        )

    barrier = pltpu.get_barrier_semaphore()
    hops = sorted({1, 2, nb - 1, nb - 2})
    for j in range(1, ns):
        pl.semaphore_signal(barrier, inc=1, device_id=(sample_peer(j), v), device_id_type=MESH)
    for j in hops:
        pl.semaphore_signal(barrier, inc=1, device_id=(s, variant_peer(j)), device_id_type=MESH)

    design[...] = jnp.zeros_like(design)
    design[0:1] = jnp.ones((1, local), F32)
    design[1:terms] = covariates[...]
    full = design[0:depth]
    high = full.astype(BF16)
    left = full - high.astype(F32)
    middle = left.astype(BF16)
    low = (left - middle.astype(F32)).astype(BF16)
    genotype = dosage[...]
    contract = ((1,), (0,))
    partial = fast_dot(high, genotype, contract) + (
        fast_dot(middle, genotype, contract) + fast_dot(low, genotype, contract)
    )
    for i in range(ns):
        r, c = divmod(i, across)
        cross_out[i] = partial[r * ROWS : (r + 1) * ROWS, c * piece : (c + 1) * piece]
    moments[s] = exact_dot(full, design[...], ((1,), (1,)))

    pl.semaphore_wait(barrier, ns - 1 + len(hops))

    sent = []

    def start(c):
        c.start()
        sent.append(c)

    for j in range(1, ns):
        p = sample_peer(j)
        start(copy(cross_out.at[p], cross_in.at[s], cross_send.at[j], cross_recv.at[j], p, v))
    for j in range(1, ns):
        p = sample_peer(j)
        start(copy(moments.at[s], moments.at[s], moment_send.at[j], moment_recv.at[j], p, v))
    behind = variant_peer(-1)
    start(copy(dosage, blocks.at[0], block_send.at[0], block_recv.at[0], s, behind))

    own_t[...] = genotype.astype(F32).T

    total = cross_out[s]
    for j in range(1, ns):
        q = sample_peer(ns - j)
        copy(cross_out.at[q], cross_in.at[q], cross_send.at[j], cross_recv.at[j], q, v).wait_recv()
        total = total + cross_in[q]
    cross_sum[s] = total
    for j in range(1, ns):
        p = sample_peer(j)
        start(copy(cross_sum.at[s], cross_sum.at[s], sum_send.at[j], sum_recv.at[j], p, v))

    moment = moments[s]
    for j in range(1, ns):
        q = sample_peer(ns - j)
        copy(moments.at[q], moments.at[q], moment_send.at[j], moment_recv.at[j], q, v).wait_recv()
        moment = moment + moments[q]
    row_at = lax.broadcasted_iota(jnp.int32, moment.shape, 0)
    lane_at = lax.broadcasted_iota(jnp.int32, moment.shape, 1)
    moment = jnp.where((row_at == lane_at) & (row_at >= terms), 1.0, moment)
    solve = inverse(moment)[:, :depth]

    for j in range(1, ns):
        q = sample_peer(ns - j)
        copy(cross_sum.at[q], cross_sum.at[q], sum_send.at[j], sum_recv.at[j], q, v).wait_recv()
    for i in range(ns):
        r, c = divmod(i, across)
        cross[r * ROWS : (r + 1) * ROWS, c * piece : (c + 1) * piece] = cross_sum[i]
    coefs[0] = exact_dot(solve, cross[...], contract)
    for k in (1, 2):
        start(copy(coefs.at[0], coefs.at[k], coef_send.at[k], coef_recv.at[k], s, variant_peer(-k)))
    copy(dosage, blocks.at[0], block_send.at[0], block_recv.at[0], s, behind).wait_recv()
    start(copy(blocks.at[0], blocks.at[1], block_send.at[1], block_recv.at[1], s, behind))

    ones = jnp.ones((ROWS, local), F32)
    mine = own_t[...] - exact_dot(coefs[0], full, ((0,), (0,)))
    own_t[...] = mine
    spreads[s, 0:1] = exact_dot(ones, mine * mine, ((1,), (1,)))[0:1]
    for k in (1, 2):
        copy(coefs.at[0], coefs.at[k], coef_send.at[k], coef_recv.at[k], s, behind).wait_recv()
        if k == 2:
            copy(blocks.at[0], blocks.at[1], block_send.at[1], block_recv.at[1], s, behind).wait_recv()
        theirs = blocks[k - 1].astype(F32) - exact_dot(full, coefs[k], ((0,), (0,)))
        spreads[s, k : k + 1] = jnp.sum(theirs * theirs, 0, keepdims=True)
        others[:, (k - 1) * width : k * width] = theirs.astype(BF16)
    spreads[s, 3:ROWS] = jnp.zeros((ROWS - 3, width), F32)
    partner = group * 2 + 1 - half
    order = list(range(1, groups)) + [0]
    for j in order:
        g = lax.rem(group + j, groups)
        lhs = own_t[pl.ds(pl.multiple_of(g * 2 * rows, 2 * rows), 2 * rows)].astype(BF16)
        tiles[j] = fast_dot(lhs, others[...], contract)
        pair_out[j] = tiles[j, pl.ds(pl.multiple_of((1 - half) * rows, rows), rows)].astype(BF16)
        start(copy(pair_out.at[j], pair_in.at[j], pair_send.at[j], pair_recv.at[j], partner, v))
    for j in range(1, ns):
        p = sample_peer(j)
        start(copy(spreads.at[s], spreads.at[s], spread_send.at[j], spread_recv.at[j], p, v))
    for j in order:
        copy(pair_out.at[j], pair_in.at[j], pair_send.at[j], pair_recv.at[j], partner, v).wait_recv()
        mine = tiles[j, pl.ds(pl.multiple_of(half * rows, rows), rows)]
        summed = mine + pair_in[j].astype(F32)
        if j:
            ring_out[j] = summed.astype(BF16)
            target = lax.rem(group + j, groups) * 2 + half
            start(copy(ring_out.at[j], ring_in.at[j], ring_send.at[j], ring_recv.at[j], target, v))

    spread = spreads[s]
    for j in range(1, ns):
        q = sample_peer(ns - j)
        copy(spreads.at[q], spreads.at[q], spread_send.at[j], spread_recv.at[j], q, v).wait_recv()
        spread = spread + spreads[q]
    samples = float(local * ns)
    scale = jnp.sqrt(samples / spread[0:3])
    chosen = lax.broadcasted_iota(jnp.int32, (rows, width), 1) == (
        lax.broadcasted_iota(jnp.int32, (rows, width), 0) + s * rows
    )
    scale_rows = jnp.sum(jnp.where(chosen, scale[0:1], 0.0), 1, keepdims=True)
    scale_rows = scale_rows * (1.0 / math.sqrt(samples))

    for j in range(1, groups):
        copy(ring_out.at[j], ring_in.at[j], ring_send.at[j], ring_recv.at[j], partner, v).wait_recv()
        summed = summed + ring_in[j].astype(F32)
    finished = []
    for k in (1, 2):
        part = summed[:, (k - 1) * width : k * width] * scale_rows * scale[k : k + 1]
        out[MAXR + k - 1] = part.astype(BF16)
        finished.append(part)

    for i in range(ns):
        turn_out[i] = jnp.concatenate(
            [part[:, i * rows : (i + 1) * rows] for part in finished], 1
        ).astype(BF16)
    for j in range(1, ns):
        p = sample_peer(j)
        start(copy(turn_out.at[p], turn_in.at[s], turn_send.at[j], turn_recv.at[j], p, v))
    turn_in[s] = turn_out[s]
    for j in range(1, ns):
        q = sample_peer(ns - j)
        copy(turn_out.at[q], turn_in.at[q], turn_send.at[j], turn_recv.at[j], q, v).wait_recv()
    turned = turn_in[...].astype(F32).reshape(width, 2 * rows).T.astype(BF16)
    ends = [k for k in (1, 2) if 2 * k % nb]
    for k in ends:
        back_out[k - 1] = turned[(k - 1) * rows : k * rows]
        start(copy(back_out.at[k - 1], back_in.at[k - 1], back_send.at[k - 1], back_recv.at[k - 1],
                   s, variant_peer(k)))
    for k in (1, 2):
        if k in ends:
            copy(back_out.at[k - 1], back_in.at[k - 1], back_send.at[k - 1], back_recv.at[k - 1],
                 s, behind).wait_recv()
            out[MAXR - k] = back_in[k - 1]
        else:
            out[MAXR - k] = finished[k - 1].astype(BF16)
    for c in sent:
        c.wait_send()


def shards(dosage, covariates, reach):
    ns, nb = lax.axis_size("sample"), lax.axis_size("variant")
    local, width = dosage.shape
    depth = -(-(covariates.shape[0] + 1) // 32) * 32
    piece = width * (depth // ROWS) // ns
    groups, rows = ns // 2, width // ns
    vmem = lambda shape, dtype: pltpu.VMEM(shape, dtype)
    pair = lambda n: [pltpu.SemaphoreType.DMA((n,))] * 2
    found = pl.pallas_call(
        functools.partial(kernel, ns, nb),
        out_shape=jax.ShapeDtypeStruct((2 * MAXR, rows, width), BF16),
        in_specs=[pl.BlockSpec(memory_space=pltpu.VMEM)] * 2,
        out_specs=pl.BlockSpec(memory_space=pltpu.VMEM),
        scratch_shapes=[
            vmem((LANES, local), F32),
            vmem((depth, width), F32),
            vmem((ns, ROWS, piece), F32),
            vmem((ns, ROWS, piece), F32),
            vmem((ns, ROWS, piece), F32),
            vmem((ns, depth, LANES), F32),
            vmem((3, depth, width), F32),
            vmem((2, local, width), BF16),
            vmem((width, local), F32),
            vmem((local, 2 * width), BF16),
            vmem((ns, ROWS, width), F32),
            vmem((groups, 2 * rows, 2 * width), F32),
            vmem((groups, rows, 2 * width), BF16),
            vmem((groups, rows, 2 * width), BF16),
            vmem((groups, rows, 2 * width), BF16),
            vmem((groups, rows, 2 * width), BF16),
            vmem((ns, rows, 2 * rows), BF16),
            vmem((ns, rows, 2 * rows), BF16),
            vmem((2, rows, width), BF16),
            vmem((2, rows, width), BF16),
            *pair(2), *pair(ns), *pair(ns), *pair(ns), *pair(3), *pair(ns), *pair(groups),
            *pair(groups), *pair(ns), *pair(2),
        ],
        compiler_params=pltpu.CompilerParams(
            collective_id=0, has_side_effects=True, vmem_limit_bytes=40 * 1024 * 1024
        ),
    )(dosage, covariates)
    distance = jnp.array([abs(m - MAXR if m < MAXR else m - MAXR + 1) for m in range(2 * MAXR)])
    live = distance <= reach[lax.axis_index("variant")]
    return jnp.where(live[:, None, None], found, jnp.zeros_like(found))


def solution(mesh):
    placed = (P("sample", "variant"), P(None, "sample"), P())
    return jax.shard_map(
        shards,
        mesh=mesh,
        in_specs=placed,
        out_specs=P(None, ("variant", "sample"), None),
        check_vma=False,
    )
```

```python
import functools
import math

import jax
import jax.numpy as jnp
from jax import lax
from jax.experimental import pallas as pl
from jax.experimental.pallas import tpu as pltpu
from jax.sharding import PartitionSpec as P

MAXR = 2
ROWS = 8
LANES = 128
MESH = pl.DeviceIdType.MESH
HIGHEST = lax.Precision.HIGHEST
F32 = jnp.float32
BF16 = jnp.bfloat16


def exact_dot(a, b, dims):
    return lax.dot_general(a, b, (dims, ((), ())), precision=HIGHEST, preferred_element_type=F32)


def pieces(x):
    high = x.astype(BF16)
    left = x - high.astype(F32)
    middle = left.astype(BF16)
    return high, middle, (left - middle.astype(F32)).astype(BF16)


def left_terms(x, axis):
    h, m, l = pieces(x)
    return jnp.concatenate([h, h, m, h, m, l], axis)


def right_terms(x, axis):
    h, m, l = pieces(x)
    return jnp.concatenate([h, m, h, l, m, h], axis)


def fast_dot(a, b, dims):
    return lax.dot_general(a, b, (dims, ((), ())), preferred_element_type=F32)


def eliminate(matrix, first, last):
    row_at = lax.broadcasted_iota(jnp.int32, matrix.shape, 0)
    lane_at = lax.broadcasted_iota(jnp.int32, matrix.shape, 1)

    def step(k, a):
        row = jnp.sum(jnp.where(row_at == k, a, 0.0), 0, keepdims=True)
        column = jnp.sum(jnp.where(lane_at == k, a, 0.0), 1, keepdims=True)
        pivot = jnp.sum(jnp.where(lane_at[:1] == k, row, 0.0), 1, keepdims=True)
        row = jnp.where(lane_at[:1] == k, 1.0, row) / pivot
        rest = jnp.where(lane_at == k, 0.0, a) - column * row
        return jnp.where(row_at == k, row, rest)

    return lax.fori_loop(first, last, step, matrix)


def kernel(
    ns, nb, dosage_in, covariates_in, reach_in, out,
    dosage, covariates, reach, design, terms_ref, cross, cross_out, cross_in, cross_sum, moments,
    coefs, blocks, own_t, own_b, others, spreads, tiles, pair_out, pair_in, ring_out, ring_in,
    turn_out, turn_in, back_out, back_in, load_sem,
    block_send, block_recv, cross_send, cross_recv, moment_send, moment_recv, sum_send, sum_recv,
    coef_send, coef_recv, spread_send, spread_recv, pair_send, pair_recv, ring_send, ring_recv,
    turn_send, turn_recv, back_send, back_recv,
):
    s = lax.axis_index("sample")
    v = lax.axis_index("variant")
    local, width = dosage.shape
    terms = covariates.shape[0] + 1
    depth = cross.shape[0]
    across = ns // (depth // ROWS)
    piece = width // across
    groups = ns // 2
    group, half = lax.div(s, 2), lax.rem(s, 2)
    rows = width // ns
    samples = float(local * ns)

    def sample_peer(j):
        return lax.rem(s + j, ns)

    def variant_peer(j):
        return lax.rem(v + j + nb, nb)

    def copy(src, dst, send, recv, sample, variant):
        return pltpu.make_async_remote_copy(
            src_ref=src, dst_ref=dst, send_sem=send, recv_sem=recv,
            device_id=(sample, variant), device_id_type=MESH,
        )

    load_dosage = pltpu.make_async_copy(dosage_in, dosage, load_sem.at[0])
    load_covariates = pltpu.make_async_copy(covariates_in, covariates, load_sem.at[1])
    load_reach = pltpu.make_async_copy(reach_in, reach, load_sem.at[2])
    load_covariates.start()
    load_dosage.start()
    load_reach.start()

    barrier = pltpu.get_barrier_semaphore()
    hops = sorted({1, 2, nb - 1, nb - 2})
    for j in range(1, ns):
        pl.semaphore_signal(barrier, inc=1, device_id=(sample_peer(j), v), device_id_type=MESH)
    for j in hops:
        pl.semaphore_signal(barrier, inc=1, device_id=(s, variant_peer(j)), device_id_type=MESH)

    sent = []

    def start(c):
        c.start()
        sent.append(c)

    contract = ((1,), (0,))
    design[...] = jnp.zeros_like(design)
    design[0:1] = jnp.ones((1, local), F32)
    load_covariates.wait()
    design[1:terms] = covariates[...]
    full = design[0:depth]
    high, middle, low = pieces(full)
    moments[s] = exact_dot(full, design[...], ((1,), (1,)))
    load_dosage.wait()
    genotype = dosage[...]
    partial = fast_dot(jnp.concatenate([high, middle, low], 0), genotype, contract)
    partial = partial[:depth] + (partial[depth : 2 * depth] + partial[2 * depth :])
    for i in range(ns):
        r, c = divmod(i, across)
        cross_out[i] = partial[r * ROWS : (r + 1) * ROWS, c * piece : (c + 1) * piece]

    pl.semaphore_wait(barrier, ns - 1 + len(hops))
    for j in range(1, ns):
        p = sample_peer(j)
        start(copy(moments.at[s], moments.at[s], moment_send.at[j], moment_recv.at[j], p, v))
        start(copy(cross_out.at[p], cross_in.at[s], cross_send.at[j], cross_recv.at[j], p, v))
    behind = variant_peer(-1)
    start(copy(dosage, blocks.at[0], block_send.at[0], block_recv.at[0], s, behind))

    terms_ref[...] = left_terms(full, 0)
    own_t[...] = genotype.astype(F32).T

    moment = moments[s]
    for j in range(1, ns):
        q = sample_peer(ns - j)
        copy(moments.at[q], moments.at[q], moment_send.at[j], moment_recv.at[j], q, v).wait_recv()
        moment = moment + moments[q]
    row_at = lax.broadcasted_iota(jnp.int32, moment.shape, 0)
    lane_at = lax.broadcasted_iota(jnp.int32, moment.shape, 1)
    moment = jnp.where((row_at == lane_at) & (row_at >= terms), 1.0, moment)
    solve = eliminate(moment, 0, depth // 4)

    total = cross_out[s]
    for j in range(1, ns):
        q = sample_peer(ns - j)
        copy(cross_out.at[q], cross_in.at[q], cross_send.at[j], cross_recv.at[j], q, v).wait_recv()
        total = total + cross_in[q]
    cross_sum[s] = total
    for j in range(1, ns):
        p = sample_peer(j)
        start(copy(cross_sum.at[s], cross_sum.at[s], sum_send.at[j], sum_recv.at[j], p, v))
    solve = eliminate(solve, depth // 4, depth)[:, :depth]

    for j in range(1, ns):
        q = sample_peer(ns - j)
        copy(cross_sum.at[q], cross_sum.at[q], sum_send.at[j], sum_recv.at[j], q, v).wait_recv()
    for i in range(ns):
        r, c = divmod(i, across)
        cross[r * ROWS : (r + 1) * ROWS, c * piece : (c + 1) * piece] = cross_sum[i]
    coefs[0] = exact_dot(solve, cross[...], contract)
    for k in (1, 2):
        start(copy(coefs.at[0], coefs.at[k], coef_send.at[k], coef_recv.at[k], s, variant_peer(-k)))
    copy(dosage, blocks.at[0], block_send.at[0], block_recv.at[0], s, behind).wait_recv()
    start(copy(blocks.at[0], blocks.at[1], block_send.at[1], block_recv.at[1], s, behind))

    mine = own_t[...] - fast_dot(right_terms(coefs[0], 0), terms_ref[...], ((0,), (0,)))
    own_b[...] = mine.astype(BF16)
    own_t[...] = mine
    partner = group * 2 + 1 - half
    order = list(range(1, groups)) + [0]

    def residual(k):
        copy(coefs.at[0], coefs.at[k], coef_send.at[k], coef_recv.at[k], s, behind).wait_recv()
        if k == 2:
            copy(blocks.at[0], blocks.at[1], block_send.at[1], block_recv.at[1], s, behind).wait_recv()
        fitted = fast_dot(terms_ref[...], right_terms(coefs[k], 0), ((0,), (0,)))
        theirs = blocks[k - 1].astype(F32) - fitted
        others[...] = theirs.astype(BF16)
        spreads[s, k : k + 1] = jnp.sum(theirs * theirs, 0, keepdims=True)

    def slot(k, j):
        return (k - 1) * groups + j

    def pair_copy(k, j):
        i = slot(k, j)
        return copy(pair_out.at[i], pair_in.at[i], pair_send.at[i], pair_recv.at[i], partner, v)

    def ring_copy(k, j):
        i = slot(k, j)
        target = lax.rem(group + j, groups) * 2 + half
        return copy(ring_out.at[i], ring_in.at[i], ring_send.at[i], ring_recv.at[i], target, v)

    def give(k, j):
        i = slot(k, j)
        g = lax.rem(group + j, groups)
        lhs = own_b[pl.ds(pl.multiple_of(g * 2 * rows, 2 * rows), 2 * rows)]
        tiles[i] = fast_dot(lhs, others[...], contract)
        pair_out[i] = tiles[i, pl.ds(pl.multiple_of((1 - half) * rows, rows), rows)].astype(BF16)
        start(pair_copy(k, j))

    def take(k, j):
        i = slot(k, j)
        pair_copy(k, j).wait_recv()
        summed = tiles[i, pl.ds(pl.multiple_of(half * rows, rows), rows)] + pair_in[i].astype(F32)
        if j:
            ring_out[i] = summed.astype(BF16)
            start(ring_copy(k, j))
        return summed

    def gather(k, summed):
        for j in range(1, groups):
            ring_copy(k, j).wait_recv()
            summed = summed + ring_in[slot(k, j)].astype(F32)
        return summed

    residual(1)
    for j in order:
        give(1, j)
    column = jnp.sum(mine * mine, 1, keepdims=True)
    spreads[s, 0:1] = jnp.broadcast_to(column, (width, LANES)).T[0:1]
    spreads[s, 3:ROWS] = jnp.zeros((ROWS - 3, width), F32)
    for j in order[:1]:
        take(1, j)
    residual(2)
    for j in range(1, ns):
        p = sample_peer(j)
        start(copy(spreads.at[s], spreads.at[s], spread_send.at[j], spread_recv.at[j], p, v))
    for n, j in enumerate(order):
        give(2, j)
        if n:
            last = take(1, j)

    spread = spreads[s]
    for j in range(1, ns):
        q = sample_peer(ns - j)
        copy(spreads.at[q], spreads.at[q], spread_send.at[j], spread_recv.at[j], q, v).wait_recv()
        spread = spread + spreads[q]
    scale = jnp.sqrt(samples / spread[0:3])
    chosen = lax.broadcasted_iota(jnp.int32, (rows, width), 1) == (
        lax.broadcasted_iota(jnp.int32, (rows, width), 0) + s * rows
    )
    scale_rows = jnp.sum(jnp.where(chosen, scale[0:1], 0.0), 1, keepdims=True)
    scale_rows = scale_rows * (1.0 / math.sqrt(samples))
    load_reach.wait()
    own_reach = reach[v]

    def masked(k, tile):
        return jnp.where(own_reach >= k, tile.astype(F32), 0.0).astype(BF16)

    def finish(k, summed):
        part = summed * scale_rows * scale[k : k + 1]
        out[MAXR + k - 1] = masked(k, part)
        return part

    def turn_copy(k, j, p, q):
        return copy(turn_out.at[k - 1, p], turn_in.at[k - 1, q], turn_send.at[(k - 1) * ns + j],
                    turn_recv.at[(k - 1) * ns + j], p, v)

    def turn_start(k, part):
        for i in range(ns):
            turn_out[k - 1, i] = part[:, i * rows : (i + 1) * rows].astype(BF16)
        for j in range(1, ns):
            start(turn_copy(k, j, sample_peer(j), s))
        turn_in[k - 1, s] = turn_out[k - 1, s]

    def back_copy(k):
        return copy(back_out.at[k - 1], back_in.at[k - 1], back_send.at[k - 1],
                    back_recv.at[k - 1], s, variant_peer(k))

    def turn_end(k):
        for j in range(1, ns):
            q = sample_peer(ns - j)
            turn_copy(k, j, q, q).wait_recv()
        back_out[k - 1] = turn_in[k - 1].astype(F32).reshape(width, rows).T.astype(BF16)
        start(back_copy(k))

    def back_end(k):
        back_copy(k).wait_recv()
        out[MAXR - k] = masked(k, back_in[k - 1])

    early = len(order) // 2
    for j in order[:early]:
        take(2, j)
    turn_start(1, finish(1, gather(1, last)))
    for j in order[early:]:
        last = take(2, j)
    turn_end(1)
    part = finish(2, gather(2, last))
    if 4 % nb:
        turn_start(2, part)
        turn_end(2)
        back_end(2)
    else:
        out[MAXR - 2] = masked(2, part)
    back_end(1)
    for c in sent:
        c.wait_send()


def shards(dosage, covariates, reach):
    ns, nb = lax.axis_size("sample"), lax.axis_size("variant")
    local, width = dosage.shape
    depth = -(-(covariates.shape[0] + 1) // 32) * 32
    piece = width * (depth // ROWS) // ns
    groups, rows = ns // 2, width // ns
    vmem = pltpu.VMEM
    pair = lambda n: [pltpu.SemaphoreType.DMA((n,))] * 2
    return pl.pallas_call(
        functools.partial(kernel, ns, nb),
        out_shape=jax.ShapeDtypeStruct((2 * MAXR, rows, width), BF16),
        in_specs=[pl.BlockSpec(memory_space=pltpu.HBM)] * 3,
        out_specs=pl.BlockSpec(memory_space=pltpu.VMEM),
        scratch_shapes=[
            vmem((local, width), BF16),
            vmem(covariates.shape, F32),
            pltpu.SMEM(reach.shape, jnp.int32),
            vmem((LANES, local), F32),
            vmem((6 * depth, local), BF16),
            vmem((depth, width), F32),
            vmem((ns, ROWS, piece), F32),
            vmem((ns, ROWS, piece), F32),
            vmem((ns, ROWS, piece), F32),
            vmem((ns, depth, LANES), F32),
            vmem((3, depth, width), F32),
            vmem((2, local, width), BF16),
            vmem((width, local), F32),
            vmem((width, local), BF16),
            vmem((local, width), BF16),
            vmem((ns, ROWS, width), F32),
            vmem((2 * groups, 2 * rows, width), F32),
            vmem((2 * groups, rows, width), BF16),
            vmem((2 * groups, rows, width), BF16),
            vmem((2 * groups, rows, width), BF16),
            vmem((2 * groups, rows, width), BF16),
            vmem((2, ns, rows, rows), BF16),
            vmem((2, ns, rows, rows), BF16),
            vmem((2, rows, width), BF16),
            vmem((2, rows, width), BF16),
            pltpu.SemaphoreType.DMA((3,)),
            *pair(2), *pair(ns), *pair(ns), *pair(ns), *pair(3), *pair(ns), *pair(2 * groups),
            *pair(2 * groups), *pair(2 * ns), *pair(2),
        ],
        compiler_params=pltpu.CompilerParams(
            collective_id=0, has_side_effects=True, vmem_limit_bytes=63 * 1024 * 1024
        ),
    )(dosage, covariates, reach)


def solution(mesh):
    placed = (P("sample", "variant"), P(None, "sample"), P())
    return jax.shard_map(
        shards,
        mesh=mesh,
        in_specs=placed,
        out_specs=P(None, ("variant", "sample"), None),
        check_vma=False,
    )
```

```python
import functools
import math

import jax
import jax.numpy as jnp
from jax import lax
from jax.experimental import pallas as pl
from jax.experimental.pallas import tpu as pltpu
from jax.sharding import PartitionSpec as P

MAXR = 2
ROWS = 8
LANES = 128
VMEM_LIMIT = 63 * 1024 * 1024
MESH = pl.DeviceIdType.MESH
HIGHEST = lax.Precision.HIGHEST
F32 = jnp.float32
BF16 = jnp.bfloat16


def exact_dot(a, b, dims):
    return lax.dot_general(a, b, (dims, ((), ())), precision=HIGHEST, preferred_element_type=F32)


def pieces(x):
    high = x.astype(BF16)
    left = x - high.astype(F32)
    middle = left.astype(BF16)
    return high, middle, (left - middle.astype(F32)).astype(BF16)


def left_terms(x, axis):
    h, m, l = pieces(x)
    return jnp.concatenate([h, h, m, h, m, l], axis)


def right_terms(x, axis):
    h, m, l = pieces(x)
    return jnp.concatenate([h, m, h, l, m, h], axis)


def fast_dot(a, b, dims):
    return lax.dot_general(a, b, (dims, ((), ())), preferred_element_type=F32)


def eliminate(matrix, first, last):
    row_at = lax.broadcasted_iota(jnp.int32, matrix.shape, 0)
    lane_at = lax.broadcasted_iota(jnp.int32, matrix.shape, 1)
    lane = lane_at[:1]
    for k in range(first, last, 2):
        one = jnp.broadcast_to(matrix[:, k : k + 1], matrix.shape)
        two = jnp.broadcast_to(matrix[:, k + 1 : k + 2], matrix.shape)
        a, c = one[k : k + 1], one[k + 1 : k + 2]
        b, d = two[k : k + 1], two[k + 1 : k + 2]
        upper = jnp.where(lane == k, 1.0, jnp.where(lane == k + 1, 0.0, matrix[k : k + 1]))
        lower = jnp.where(lane == k, 0.0, jnp.where(lane == k + 1, 1.0, matrix[k + 1 : k + 2]))
        ratio = c / a
        lower = (lower - ratio * upper) / (d - ratio * b)
        upper = (upper - b * lower) / a
        rest = jnp.where((lane_at == k) | (lane_at == k + 1), 0.0, matrix)
        rest = rest - one * upper - two * lower
        matrix = jnp.where(row_at == k, upper, jnp.where(row_at == k + 1, lower, rest))
    return matrix


def kernel(
    ns, nb, dosage_in, covariates_in, reach_in, out,
    dosage, covariates, reach, design, terms_ref, cross, cross_out, cross_in, cross_sum, moments,
    blocks, own_t, own_b, spreads, tiles, pair_out, pair_in, ring_out, ring_in,
    turn_out, turn_in, back_out, back_in, load_sem,
    block_send, block_recv, cross_send, cross_recv, moment_send, moment_recv, sum_send, sum_recv,
    spread_send, spread_recv, pair_send, pair_recv, ring_send, ring_recv,
    turn_send, turn_recv, back_send, back_recv,
):
    s = lax.axis_index("sample")
    v = lax.axis_index("variant")
    local, width = dosage.shape
    terms = covariates.shape[0] + 1
    depth = cross.shape[1]
    across = ns // (depth // ROWS)
    piece = width // across
    groups = ns // 2
    group, half = lax.div(s, 2), lax.rem(s, 2)
    rows = width // ns
    samples = float(local * ns)

    def sample_peer(j):
        return lax.rem(s + j, ns)

    def variant_peer(j):
        return lax.rem(v + j + nb, nb)

    def copy(src, dst, send, recv, sample, variant):
        return pltpu.make_async_remote_copy(
            src_ref=src, dst_ref=dst, send_sem=send, recv_sem=recv,
            device_id=(sample, variant), device_id_type=MESH,
        )

    load_dosage = pltpu.make_async_copy(dosage_in, dosage, load_sem.at[0])
    load_covariates = pltpu.make_async_copy(covariates_in, covariates, load_sem.at[1])
    load_reach = pltpu.make_async_copy(reach_in, reach, load_sem.at[2])
    load_covariates.start()
    load_dosage.start()
    load_reach.start()

    barrier = pltpu.get_barrier_semaphore()
    hops = sorted({1, 2, nb - 1, nb - 2})
    for j in range(1, ns):
        pl.semaphore_signal(barrier, inc=1, device_id=(sample_peer(j), v), device_id_type=MESH)
    for h in hops:
        for j in range(ns):
            pl.semaphore_signal(
                barrier, inc=1, device_id=(sample_peer(j), variant_peer(h)), device_id_type=MESH
            )

    sent = []

    def start(c):
        c.start()
        sent.append(c)

    contract = ((1,), (0,))
    design[...] = jnp.zeros_like(design)
    design[0:1] = jnp.ones((1, local), F32)
    load_covariates.wait()
    design[1:terms] = covariates[...]
    full = design[0:depth]
    high, middle, low = pieces(full)
    moments[s] = exact_dot(full, design[...], ((1,), (1,)))
    load_dosage.wait()
    genotype = dosage[...]
    partial = fast_dot(jnp.concatenate([high, middle, low], 0), genotype, contract)
    partial = partial[:depth] + (partial[depth : 2 * depth] + partial[2 * depth :])
    for i in range(ns):
        r, c = divmod(i, across)
        cross_out[i] = partial[r * ROWS : (r + 1) * ROWS, c * piece : (c + 1) * piece]

    pl.semaphore_wait(barrier, ns - 1 + ns * len(hops))
    for j in range(1, ns):
        p = sample_peer(j)
        start(copy(moments.at[s], moments.at[s], moment_send.at[j], moment_recv.at[j], p, v))
        start(copy(cross_out.at[p], cross_in.at[s], cross_send.at[j], cross_recv.at[j], p, v))
    behind = variant_peer(-1)
    start(copy(dosage, blocks.at[0], block_send.at[0], block_recv.at[0], s, behind))

    terms_ref[...] = left_terms(full, 0)
    own_t[...] = genotype.astype(F32).T

    moment = moments[s]
    for j in range(1, ns):
        q = sample_peer(ns - j)
        copy(moments.at[q], moments.at[q], moment_send.at[j], moment_recv.at[j], q, v).wait_recv()
        moment = moment + moments[q]
    row_at = lax.broadcasted_iota(jnp.int32, moment.shape, 0)
    lane_at = lax.broadcasted_iota(jnp.int32, moment.shape, 1)
    moment = jnp.where((row_at == lane_at) & (row_at >= terms), 1.0, moment)
    solve = eliminate(moment, 0, depth // 4)

    total = cross_out[s]
    for j in range(1, ns):
        q = sample_peer(ns - j)
        copy(cross_out.at[q], cross_in.at[q], cross_send.at[j], cross_recv.at[j], q, v).wait_recv()
        total = total + cross_in[q]
    cross_sum[0, s] = total

    def sum_copy(k, j, slot, p):
        return copy(cross_sum.at[0, s], cross_sum.at[k, slot], sum_send.at[k * ns + j],
                    sum_recv.at[k * ns + j], p, variant_peer(-k))

    for j in range(1, ns):
        start(sum_copy(0, j, s, sample_peer(j)))
    for k in (1, 2):
        for j in range(ns):
            start(sum_copy(k, j, s, sample_peer(j)))
    solve = eliminate(solve, depth // 4, depth)[:, :depth]
    copy(dosage, blocks.at[0], block_send.at[0], block_recv.at[0], s, behind).wait_recv()
    start(copy(blocks.at[0], blocks.at[1], block_send.at[1], block_recv.at[1], s, behind))

    def coefficients(k):
        for j in range(1 if k == 0 else 0, ns):
            q = sample_peer(ns - j)
            sum_copy(k, j, q, q).wait_recv()
        for i in range(ns):
            r, c = divmod(i, across)
            cross[k, r * ROWS : (r + 1) * ROWS, c * piece : (c + 1) * piece] = cross_sum[k, i]
        return right_terms(exact_dot(solve, cross[k], contract), 0)

    mine = own_t[...] - fast_dot(coefficients(0), terms_ref[...], ((0,), (0,)))
    own_b[...] = mine.astype(BF16)
    own_t[...] = mine
    partner = group * 2 + 1 - half
    order = list(range(1, groups)) + [0]

    def residual(k):
        if k == 2:
            copy(blocks.at[0], blocks.at[1], block_send.at[1], block_recv.at[1], s, behind).wait_recv()
        fitted = fast_dot(terms_ref[...], coefficients(k), ((0,), (0,)))
        theirs = blocks[k - 1].astype(F32) - fitted
        tiles[k - 1] = fast_dot(own_b[...], theirs.astype(BF16), contract)
        spreads[s, k : k + 1] = jnp.sum(theirs * theirs, 0, keepdims=True)

    def slot(k, j):
        return (k - 1) * groups + j

    def pair_copy(k, j):
        i = slot(k, j)
        return copy(pair_out.at[i], pair_in.at[i], pair_send.at[i], pair_recv.at[i], partner, v)

    def ring_copy(k, j):
        i = slot(k, j)
        target = lax.rem(group + j, groups) * 2 + half
        return copy(ring_out.at[i], ring_in.at[i], ring_send.at[i], ring_recv.at[i], target, v)

    def give(k, j):
        i = slot(k, j)
        g = lax.rem(group + j, groups)
        at = pl.multiple_of((g * 2 + 1 - half) * rows, rows)
        pair_out[i] = tiles[k - 1, pl.ds(at, rows)].astype(BF16)
        start(pair_copy(k, j))

    def take(k, j):
        i = slot(k, j)
        pair_copy(k, j).wait_recv()
        g = lax.rem(group + j, groups)
        at = pl.multiple_of((g * 2 + half) * rows, rows)
        summed = tiles[k - 1, pl.ds(at, rows)] + pair_in[i].astype(F32)
        if j:
            ring_out[i] = summed.astype(BF16)
            start(ring_copy(k, j))
        return summed

    def gather(k, summed):
        for j in range(1, groups):
            ring_copy(k, j).wait_recv()
            summed = summed + ring_in[slot(k, j)].astype(F32)
        return summed

    residual(1)
    for j in order:
        give(1, j)
    column = jnp.sum(mine * mine, 1, keepdims=True)
    spreads[s, 0:1] = jnp.broadcast_to(column, (width, LANES)).T[0:1]
    spreads[s, 3:ROWS] = jnp.zeros((ROWS - 3, width), F32)
    for j in order[:1]:
        take(1, j)
    residual(2)
    for j in range(1, ns):
        p = sample_peer(j)
        start(copy(spreads.at[s], spreads.at[s], spread_send.at[j], spread_recv.at[j], p, v))
    for n, j in enumerate(order):
        give(2, j)
        if n:
            last = take(1, j)

    spread = spreads[s]
    for j in range(1, ns):
        q = sample_peer(ns - j)
        copy(spreads.at[q], spreads.at[q], spread_send.at[j], spread_recv.at[j], q, v).wait_recv()
        spread = spread + spreads[q]
    scale = jnp.sqrt(samples / spread[0:3])
    chosen = lax.broadcasted_iota(jnp.int32, (rows, width), 1) == (
        lax.broadcasted_iota(jnp.int32, (rows, width), 0) + s * rows
    )
    scale_rows = jnp.sum(jnp.where(chosen, scale[0:1], 0.0), 1, keepdims=True)
    scale_rows = scale_rows * (1.0 / math.sqrt(samples))
    load_reach.wait()
    own_reach = reach[v]

    def masked(k, tile):
        return jnp.where(own_reach >= k, tile.astype(F32), 0.0).astype(BF16)

    def finish(k, summed):
        part = summed * scale_rows * scale[k : k + 1]
        out[MAXR + k - 1] = masked(k, part)
        return part

    def turn_copy(k, j, p, q):
        return copy(turn_out.at[k - 1, p], turn_in.at[k - 1, q], turn_send.at[(k - 1) * ns + j],
                    turn_recv.at[(k - 1) * ns + j], p, v)

    def turn_start(k, part):
        for i in range(ns):
            turn_out[k - 1, i] = part[:, i * rows : (i + 1) * rows].astype(BF16)
        for j in range(1, ns):
            start(turn_copy(k, j, sample_peer(j), s))
        turn_in[k - 1, s] = turn_out[k - 1, s]

    def back_copy(k):
        return copy(back_out.at[k - 1], back_in.at[k - 1], back_send.at[k - 1],
                    back_recv.at[k - 1], s, variant_peer(k))

    def turn_end(k):
        for j in range(1, ns):
            q = sample_peer(ns - j)
            turn_copy(k, j, q, q).wait_recv()
        back_out[k - 1] = turn_in[k - 1].astype(F32).reshape(width, rows).T.astype(BF16)
        start(back_copy(k))

    def back_end(k):
        back_copy(k).wait_recv()
        out[MAXR - k] = masked(k, back_in[k - 1])

    early = len(order) // 2
    for j in order[:early]:
        take(2, j)
    turn_start(1, finish(1, gather(1, last)))
    for j in order[early:]:
        last = take(2, j)
    turn_end(1)
    part = finish(2, gather(2, last))
    if 4 % nb:
        turn_start(2, part)
        turn_end(2)
        back_end(2)
    else:
        out[MAXR - 2] = masked(2, part)
    back_end(1)
    for c in sent:
        c.wait_send()


def shards(dosage, covariates, reach):
    ns, nb = lax.axis_size("sample"), lax.axis_size("variant")
    local, width = dosage.shape
    depth = -(-(covariates.shape[0] + 1) // 32) * 32
    piece = width * (depth // ROWS) // ns
    groups, rows = ns // 2, width // ns
    vmem = pltpu.VMEM
    pair = lambda n: [pltpu.SemaphoreType.DMA((n,))] * 2
    return pl.pallas_call(
        functools.partial(kernel, ns, nb),
        out_shape=jax.ShapeDtypeStruct((2 * MAXR, rows, width), BF16),
        in_specs=[pl.BlockSpec(memory_space=pltpu.HBM)] * 3,
        out_specs=pl.BlockSpec(memory_space=pltpu.VMEM),
        scratch_shapes=[
            vmem((local, width), BF16),
            vmem(covariates.shape, F32),
            pltpu.SMEM(reach.shape, jnp.int32),
            vmem((LANES, local), F32),
            vmem((6 * depth, local), BF16),
            vmem((3, depth, width), F32),
            vmem((ns, ROWS, piece), F32),
            vmem((ns, ROWS, piece), F32),
            vmem((3, ns, ROWS, piece), F32),
            vmem((ns, depth, LANES), F32),
            vmem((2, local, width), BF16),
            vmem((width, local), F32),
            vmem((width, local), BF16),
            vmem((ns, ROWS, width), F32),
            vmem((2, width, width), F32),
            vmem((2 * groups, rows, width), BF16),
            vmem((2 * groups, rows, width), BF16),
            vmem((2 * groups, rows, width), BF16),
            vmem((2 * groups, rows, width), BF16),
            vmem((2, ns, rows, rows), BF16),
            vmem((2, ns, rows, rows), BF16),
            vmem((2, rows, width), BF16),
            vmem((2, rows, width), BF16),
            pltpu.SemaphoreType.DMA((3,)),
            *pair(2), *pair(ns), *pair(ns), *pair(3 * ns), *pair(ns), *pair(2 * groups),
            *pair(2 * groups), *pair(2 * ns), *pair(2),
        ],
        compiler_params=pltpu.CompilerParams(
            collective_id=0, has_side_effects=True, vmem_limit_bytes=VMEM_LIMIT
        ),
    )(dosage, covariates, reach)


def solution(mesh):
    placed = (P("sample", "variant"), P(None, "sample"), P())
    return jax.shard_map(
        shards,
        mesh=mesh,
        in_specs=placed,
        out_specs=P(None, ("variant", "sample"), None),
        check_vma=False,
    )
```

```python
import functools
import math

import jax
import jax.numpy as jnp
from jax import lax
from jax.experimental import pallas as pl
from jax.experimental.pallas import tpu as pltpu
from jax.sharding import PartitionSpec as P

MAXR = 2
ROWS = 8
LANES = 128
VMEM_LIMIT = 63 * 1024 * 1024
MESH = pl.DeviceIdType.MESH
HIGHEST = lax.Precision.HIGHEST
F32 = jnp.float32
BF16 = jnp.bfloat16


def exact_dot(a, b, dims):
    return lax.dot_general(a, b, (dims, ((), ())), precision=HIGHEST, preferred_element_type=F32)


def pieces(x):
    high = x.astype(BF16)
    left = x - high.astype(F32)
    middle = left.astype(BF16)
    return high, middle, (left - middle.astype(F32)).astype(BF16)


def left_terms(x, axis):
    h, m, l = pieces(x)
    return jnp.concatenate([h, h, m, h, m, l], axis)


def right_terms(x, axis):
    h, m, l = pieces(x)
    return jnp.concatenate([h, m, h, l, m, h], axis)


def fast_dot(a, b, dims):
    return lax.dot_general(a, b, (dims, ((), ())), preferred_element_type=F32)


def eliminate(matrix, first, last):
    row_at = lax.broadcasted_iota(jnp.int32, matrix.shape, 0)
    lane_at = lax.broadcasted_iota(jnp.int32, matrix.shape, 1)
    lane = lane_at[:1]
    for k in range(first, last, 2):
        one = jnp.broadcast_to(matrix[:, k : k + 1], matrix.shape)
        two = jnp.broadcast_to(matrix[:, k + 1 : k + 2], matrix.shape)
        a, c = one[k : k + 1], one[k + 1 : k + 2]
        b, d = two[k : k + 1], two[k + 1 : k + 2]
        upper = jnp.where(lane == k, 1.0, jnp.where(lane == k + 1, 0.0, matrix[k : k + 1]))
        lower = jnp.where(lane == k, 0.0, jnp.where(lane == k + 1, 1.0, matrix[k + 1 : k + 2]))
        ratio = c / a
        lower = (lower - ratio * upper) / (d - ratio * b)
        upper = (upper - b * lower) / a
        rest = jnp.where((lane_at == k) | (lane_at == k + 1), 0.0, matrix)
        rest = rest - one * upper - two * lower
        matrix = jnp.where(row_at == k, upper, jnp.where(row_at == k + 1, lower, rest))
    return matrix


def kernel(
    ns, nb, dosage_in, covariates_in, reach_in, out,
    dosage, covariates, reach, design, terms_ref, cross, cross_out, cross_in, cross_sum, coefs,
    blocks, own_t, own_b, spreads, tiles, pair_out, pair_in, ring_out, ring_in,
    turn_out, turn_in, back_out, back_in, load_sem,
    block_send, block_recv, cross_send, cross_recv, sum_send, sum_recv, coef_send, coef_recv,
    spread_send, spread_recv, pair_send, pair_recv, ring_send, ring_recv,
    turn_send, turn_recv, back_send, back_recv,
):
    s = lax.axis_index("sample")
    v = lax.axis_index("variant")
    local, width = dosage.shape
    terms = covariates.shape[0] + 1
    depth = cross.shape[0]
    across = ns // (depth // ROWS)
    piece = width // across
    groups = ns // 2
    group, half = lax.div(s, 2), lax.rem(s, 2)
    rows = width // ns
    samples = float(local * ns)

    def sample_peer(j):
        return lax.rem(s + j, ns)

    def variant_peer(j):
        return lax.rem(v + j + nb, nb)

    def copy(src, dst, send, recv, sample, variant):
        return pltpu.make_async_remote_copy(
            src_ref=src, dst_ref=dst, send_sem=send, recv_sem=recv,
            device_id=(sample, variant), device_id_type=MESH,
        )

    load_dosage = pltpu.make_async_copy(dosage_in, dosage, load_sem.at[0])
    load_covariates = pltpu.make_async_copy(covariates_in, covariates, load_sem.at[1])
    load_reach = pltpu.make_async_copy(reach_in, reach, load_sem.at[2])
    load_covariates.start()
    load_dosage.start()
    load_reach.start()

    barrier = pltpu.get_barrier_semaphore()
    hops = sorted({1, 2, nb - 1, nb - 2})
    for j in range(1, ns):
        pl.semaphore_signal(barrier, inc=1, device_id=(sample_peer(j), v), device_id_type=MESH)
    for j in hops:
        pl.semaphore_signal(barrier, inc=1, device_id=(s, variant_peer(j)), device_id_type=MESH)

    sent = []

    def flush(count):
        for c in sent[:count]:
            c.wait_send()
        del sent[:count]

    def start(c):
        c.start()
        sent.append(c)

    contract = ((1,), (0,))
    design[...] = jnp.zeros_like(design)
    design[0:1] = jnp.ones((1, local), F32)
    load_covariates.wait()
    design[1:terms] = covariates[...]
    full = design[0:depth]
    high, middle, low = pieces(full)
    moment = exact_dot(full, design[...], ((1,), (1,)))[:, :depth]
    packed = jnp.concatenate([moment[r : r + ROWS] for r in range(0, depth, ROWS)], 1)
    load_dosage.wait()
    genotype = dosage[...]
    partial = fast_dot(jnp.concatenate([high, middle, low], 0), genotype, contract)
    partial = partial[:depth] + (partial[depth : 2 * depth] + partial[2 * depth :])
    for i in range(ns):
        r, c = divmod(i, across)
        cross_out[i, :, :piece] = partial[r * ROWS : (r + 1) * ROWS, c * piece : (c + 1) * piece]
        cross_out[i, :, piece:] = packed

    pl.semaphore_wait(barrier, ns - 1 + len(hops))
    behind = variant_peer(-1)
    start(copy(dosage, blocks.at[0], block_send.at[0], block_recv.at[0], s, behind))
    for j in range(1, ns):
        p = sample_peer(j)
        start(copy(cross_out.at[p], cross_in.at[s], cross_send.at[j], cross_recv.at[j], p, v))
    terms_ref[...] = left_terms(full, 0)
    own_t[...] = genotype.astype(F32).T

    total = cross_out[s]
    for j in range(1, ns):
        q = sample_peer(ns - j)
        copy(cross_out.at[q], cross_in.at[q], cross_send.at[j], cross_recv.at[j], q, v).wait_recv()
        total = total + cross_in[q]
    cross_sum[s] = total[:, :piece]

    def sum_copy(j, slot, p):
        return copy(cross_sum.at[s], cross_sum.at[slot], sum_send.at[j], sum_recv.at[j], p, v)

    for j in range(1, ns):
        start(sum_copy(j, s, sample_peer(j)))
    packed = total[:, piece:]
    shares = [packed[:, r * depth : (r + 1) * depth] for r in range(depth // ROWS)]
    moment = jnp.concatenate(shares, 0)
    row_at = lax.broadcasted_iota(jnp.int32, moment.shape, 0)
    lane_at = lax.broadcasted_iota(jnp.int32, moment.shape, 1)
    moment = jnp.where((row_at == lane_at) & (row_at >= terms), 1.0, moment)
    solve = eliminate(moment, 0, depth)
    for j in range(1, ns):
        q = sample_peer(ns - j)
        sum_copy(j, q, q).wait_recv()
    for i in range(ns):
        r, c = divmod(i, across)
        cross[r * ROWS : (r + 1) * ROWS, c * piece : (c + 1) * piece] = cross_sum[i]
    coefs[0] = exact_dot(solve, cross[...], contract)

    def coef_copy(k):
        return copy(coefs.at[0], coefs.at[k], coef_send.at[k], coef_recv.at[k], s, variant_peer(-k))

    for k in (1, 2):
        start(coef_copy(k))
    copy(dosage, blocks.at[0], block_send.at[0], block_recv.at[0], s, behind).wait_recv()
    start(copy(blocks.at[0], blocks.at[1], block_send.at[1], block_recv.at[1], s, behind))

    mine = own_t[...] - fast_dot(right_terms(coefs[0], 0), terms_ref[...], ((0,), (0,)))
    own_b[...] = mine.astype(BF16)
    own_t[...] = mine
    partner = group * 2 + 1 - half
    order = list(range(1, groups)) + [0]

    def store_spread(k, values):
        spreads[s, k : k + 1] = values[:, : width // 2]
        spreads[s, k + 3 : k + 4] = values[:, width // 2 :]

    def residual(k):
        coef_copy(k).wait_recv()
        if k == 2:
            copy(blocks.at[0], blocks.at[1], block_send.at[1], block_recv.at[1], s, behind).wait_recv()
        fitted = fast_dot(terms_ref[...], right_terms(coefs[k], 0), ((0,), (0,)))
        theirs = blocks[k - 1].astype(F32) - fitted
        tiles[k - 1] = fast_dot(own_b[...], theirs.astype(BF16), contract)
        store_spread(k, jnp.sum(theirs * theirs, 0, keepdims=True))

    def slot(k, j):
        return (k - 1) * groups + j

    def pair_copy(k, j):
        i = slot(k, j)
        return copy(pair_out.at[i], pair_in.at[i], pair_send.at[i], pair_recv.at[i], partner, v)

    def ring_copy(k, j):
        i = slot(k, j)
        target = lax.rem(group + j, groups) * 2 + half
        return copy(ring_out.at[i], ring_in.at[i], ring_send.at[i], ring_recv.at[i], target, v)

    def give(k, j):
        i = slot(k, j)
        g = lax.rem(group + j, groups)
        at = pl.multiple_of((g * 2 + 1 - half) * rows, rows)
        pair_out[i] = tiles[k - 1, pl.ds(at, rows)].astype(BF16)
        start(pair_copy(k, j))

    def take(k, j):
        i = slot(k, j)
        pair_copy(k, j).wait_recv()
        g = lax.rem(group + j, groups)
        at = pl.multiple_of((g * 2 + half) * rows, rows)
        summed = tiles[k - 1, pl.ds(at, rows)] + pair_in[i].astype(F32)
        if j:
            ring_out[i] = summed.astype(BF16)
            start(ring_copy(k, j))
        return summed

    def gather(k, summed):
        for j in range(1, groups):
            ring_copy(k, j).wait_recv()
            summed = summed + ring_in[slot(k, j)].astype(F32)
        return summed

    residual(1)
    early_sends = len(sent)
    for j in order:
        give(1, j)
    column = jnp.sum(mine * mine, 1, keepdims=True)
    store_spread(0, jnp.broadcast_to(column, (width, LANES)).T[0:1])
    spreads[s, 6:ROWS] = jnp.zeros((ROWS - 6, width // 2), F32)
    for j in order[:1]:
        take(1, j)
    flush(early_sends)
    residual(2)
    for j in range(1, ns):
        p = sample_peer(j)
        start(copy(spreads.at[s], spreads.at[s], spread_send.at[j], spread_recv.at[j], p, v))
    for n, j in enumerate(order):
        give(2, j)
        if n:
            last = take(1, j)

    middle_sends = len(sent)
    spread = spreads[s]
    for j in range(1, ns):
        q = sample_peer(ns - j)
        copy(spreads.at[q], spreads.at[q], spread_send.at[j], spread_recv.at[j], q, v).wait_recv()
        spread = spread + spreads[q]
    scale = jnp.sqrt(samples / jnp.concatenate([spread[0:3], spread[3:6]], 1))
    chosen = lax.broadcasted_iota(jnp.int32, (rows, width), 1) == (
        lax.broadcasted_iota(jnp.int32, (rows, width), 0) + s * rows
    )
    scale_rows = jnp.sum(jnp.where(chosen, scale[0:1], 0.0), 1, keepdims=True)
    scale_rows = scale_rows * (1.0 / math.sqrt(samples))
    load_reach.wait()
    own_reach = reach[v]

    def masked(k, tile):
        return jnp.where(own_reach >= k, tile.astype(F32), 0.0).astype(BF16)

    def finish(k, summed):
        part = summed * scale_rows * scale[k : k + 1]
        out[MAXR + k - 1] = masked(k, part)
        return part

    def turn_copy(k, j, p, q):
        return copy(turn_out.at[k - 1, p], turn_in.at[k - 1, q], turn_send.at[(k - 1) * ns + j],
                    turn_recv.at[(k - 1) * ns + j], p, v)

    def turn_start(k, part):
        for i in range(ns):
            turn_out[k - 1, i] = part[:, i * rows : (i + 1) * rows].astype(BF16)
        for j in range(1, ns):
            start(turn_copy(k, j, sample_peer(j), s))
        turn_in[k - 1, s] = turn_out[k - 1, s]

    def back_copy(k):
        return copy(back_out.at[k - 1], back_in.at[k - 1], back_send.at[k - 1],
                    back_recv.at[k - 1], s, variant_peer(k))

    def turn_end(k):
        for j in range(1, ns):
            q = sample_peer(ns - j)
            turn_copy(k, j, q, q).wait_recv()
        back_out[k - 1] = turn_in[k - 1].astype(F32).reshape(width, rows).T.astype(BF16)
        start(back_copy(k))

    def back_end(k):
        back_copy(k).wait_recv()
        out[MAXR - k] = masked(k, back_in[k - 1])

    early = len(order) // 2
    for j in order[:early]:
        take(2, j)
    turn_start(1, finish(1, gather(1, last)))
    for j in order[early:]:
        last = take(2, j)
    flush(middle_sends)
    turn_end(1)
    part = finish(2, gather(2, last))
    if 4 % nb:
        turn_start(2, part)
        turn_end(2)
        back_end(2)
    else:
        out[MAXR - 2] = masked(2, part)
    back_end(1)
    flush(len(sent))


def shards(dosage, covariates, reach):
    ns, nb = lax.axis_size("sample"), lax.axis_size("variant")
    local, width = dosage.shape
    depth = -(-(covariates.shape[0] + 1) // 32) * 32
    piece = width * (depth // ROWS) // ns
    groups, rows = ns // 2, width // ns
    vmem = pltpu.VMEM
    pair = lambda n: [pltpu.SemaphoreType.DMA((n,))] * 2
    return pl.pallas_call(
        functools.partial(kernel, ns, nb),
        out_shape=jax.ShapeDtypeStruct((2 * MAXR, rows, width), BF16),
        in_specs=[pl.BlockSpec(memory_space=pltpu.HBM)] * 3,
        out_specs=pl.BlockSpec(memory_space=pltpu.VMEM),
        scratch_shapes=[
            vmem((local, width), BF16),
            vmem(covariates.shape, F32),
            pltpu.SMEM(reach.shape, jnp.int32),
            vmem((LANES, local), F32),
            vmem((6 * depth, local), BF16),
            vmem((depth, width), F32),
            vmem((ns, ROWS, piece + LANES), F32),
            vmem((ns, ROWS, piece + LANES), F32),
            vmem((ns, ROWS, piece), F32),
            vmem((3, depth, width), F32),
            vmem((2, local, width), BF16),
            vmem((width, local), F32),
            vmem((width, local), BF16),
            vmem((ns, ROWS, width // 2), F32),
            vmem((2, width, width), F32),
            vmem((2 * groups, rows, width), BF16),
            vmem((2 * groups, rows, width), BF16),
            vmem((2 * groups, rows, width), BF16),
            vmem((2 * groups, rows, width), BF16),
            vmem((2, ns, rows, rows), BF16),
            vmem((2, ns, rows, rows), BF16),
            vmem((2, rows, width), BF16),
            vmem((2, rows, width), BF16),
            pltpu.SemaphoreType.DMA((3,)),
            *pair(2), *pair(ns), *pair(ns), *pair(3), *pair(ns), *pair(2 * groups),
            *pair(2 * groups), *pair(2 * ns), *pair(2),
        ],
        compiler_params=pltpu.CompilerParams(
            collective_id=0, has_side_effects=True, vmem_limit_bytes=VMEM_LIMIT
        ),
    )(dosage, covariates, reach)


def solution(mesh):
    placed = (P("sample", "variant"), P(None, "sample"), P())
    return jax.shard_map(
        shards,
        mesh=mesh,
        in_specs=placed,
        out_specs=P(None, ("variant", "sample"), None),
        check_vma=False,
    )
```

```python
import functools
import math

import jax
import jax.numpy as jnp
from jax import lax
from jax.experimental import pallas as pl
from jax.experimental.pallas import tpu as pltpu
from jax.sharding import PartitionSpec as P

MAXR = 2
ROWS = 8
LANES = 128
VMEM_LIMIT = 63 * 1024 * 1024
MESH = pl.DeviceIdType.MESH
HIGHEST = lax.Precision.HIGHEST
F32 = jnp.float32
BF16 = jnp.bfloat16


def exact_dot(a, b, dims):
    return lax.dot_general(a, b, (dims, ((), ())), precision=HIGHEST, preferred_element_type=F32)


def pieces(x):
    high = x.astype(BF16)
    left = x - high.astype(F32)
    middle = left.astype(BF16)
    return high, middle, (left - middle.astype(F32)).astype(BF16)


def left_terms(x, axis):
    h, m, l = pieces(x)
    return jnp.concatenate([h, h, m, h, m, l], axis)


def right_terms(x, axis):
    h, m, l = pieces(x)
    return jnp.concatenate([h, m, h, l, m, h], axis)


def fast_dot(a, b, dims):
    return lax.dot_general(a, b, (dims, ((), ())), preferred_element_type=F32)


def eliminate(matrix, first, last):
    row_at = lax.broadcasted_iota(jnp.int32, matrix.shape, 0)
    lane_at = lax.broadcasted_iota(jnp.int32, matrix.shape, 1)
    lane = lane_at[:1]
    for k in range(first, last, 2):
        one = jnp.broadcast_to(matrix[:, k : k + 1], matrix.shape)
        two = jnp.broadcast_to(matrix[:, k + 1 : k + 2], matrix.shape)
        a, c = one[k : k + 1], one[k + 1 : k + 2]
        b, d = two[k : k + 1], two[k + 1 : k + 2]
        upper = jnp.where(lane == k, 1.0, jnp.where(lane == k + 1, 0.0, matrix[k : k + 1]))
        lower = jnp.where(lane == k, 0.0, jnp.where(lane == k + 1, 1.0, matrix[k + 1 : k + 2]))
        ratio = c / a
        lower = (lower - ratio * upper) / (d - ratio * b)
        upper = (upper - b * lower) / a
        rest = jnp.where((lane_at == k) | (lane_at == k + 1), 0.0, matrix)
        rest = rest - one * upper - two * lower
        matrix = jnp.where(row_at == k, upper, jnp.where(row_at == k + 1, lower, rest))
    return matrix


def kernel(
    ns, nb, dosage_in, covariates_in, reach_in, out,
    dosage, covariates, reach, design, terms_ref, cross, cross_out, cross_in, cross_sum, coefs,
    blocks, own_t, own_b, spreads, tiles, pair_out, pair_in, ring_out, ring_in,
    turn_out, turn_in, back_out, back_in, load_sem,
    block_send, block_recv, cross_send, cross_recv, sum_send, sum_recv, coef_send, coef_recv,
    spread_send, spread_recv, pair_send, pair_recv, ring_send, ring_recv,
    turn_send, turn_recv, back_send, back_recv,
):
    s = lax.axis_index("sample")
    v = lax.axis_index("variant")
    local, width = dosage.shape
    terms = covariates.shape[0] + 1
    depth = cross.shape[0]
    across = ns // (depth // ROWS)
    piece = width // across
    groups = ns // 2
    group, half = lax.div(s, 2), lax.rem(s, 2)
    rows = width // ns
    samples = float(local * ns)

    def sample_peer(j):
        return lax.rem(s + j, ns)

    def variant_peer(j):
        return lax.rem(v + j + nb, nb)

    def copy(src, dst, send, recv, sample, variant):
        return pltpu.make_async_remote_copy(
            src_ref=src, dst_ref=dst, send_sem=send, recv_sem=recv,
            device_id=(sample, variant), device_id_type=MESH,
        )

    load_dosage = pltpu.make_async_copy(dosage_in, dosage, load_sem.at[0])
    load_covariates = pltpu.make_async_copy(covariates_in, covariates, load_sem.at[1])
    load_reach = pltpu.make_async_copy(reach_in, reach, load_sem.at[2])
    load_covariates.start()
    load_dosage.start()
    load_reach.start()

    barrier = pltpu.get_barrier_semaphore()
    hops = sorted({1, 2, nb - 1, nb - 2})
    for j in range(1, ns):
        pl.semaphore_signal(barrier, inc=1, device_id=(sample_peer(j), v), device_id_type=MESH)
    for j in hops:
        pl.semaphore_signal(barrier, inc=1, device_id=(s, variant_peer(j)), device_id_type=MESH)

    sent = []

    def flush(count):
        for c in sent[:count]:
            c.wait_send()
        del sent[:count]

    def start(c):
        c.start()
        sent.append(c)

    contract = ((1,), (0,))
    design[...] = jnp.zeros_like(design)
    design[0:1] = jnp.ones((1, local), F32)
    load_covariates.wait()
    design[1:terms] = covariates[...]
    full = design[0:depth]
    high, middle, low = pieces(full)
    moment = exact_dot(full, design[...], ((1,), (1,)))[:, :depth]
    packed = jnp.concatenate([moment[r : r + ROWS] for r in range(0, depth, ROWS)], 1)
    load_dosage.wait()
    genotype = dosage[...]
    partial = fast_dot(jnp.concatenate([high, middle, low], 0), genotype, contract)
    partial = partial[:depth] + (partial[depth : 2 * depth] + partial[2 * depth :])
    for i in range(ns):
        r, c = divmod(i, across)
        cross_out[i, :, :piece] = partial[r * ROWS : (r + 1) * ROWS, c * piece : (c + 1) * piece]
        cross_out[i, :, piece:] = packed

    pl.semaphore_wait(barrier, ns - 1 + len(hops))
    behind = variant_peer(-1)
    for j in range(1, ns):
        p = sample_peer(j)
        start(copy(cross_out.at[p], cross_in.at[s], cross_send.at[j], cross_recv.at[j], p, v))

    def block_copy(k, part):
        at = pl.ds(part * (local // 2), local // 2)
        src = dosage if k == 1 else blocks.at[0]
        i = (k - 1) * 2 + part
        return copy(src.at[at], blocks.at[k - 1, at], block_send.at[i], block_recv.at[i], s, behind)

    for part in (0, 1):
        start(block_copy(1, part))
    terms_ref[...] = left_terms(full, 0)
    own_t[...] = genotype.astype(F32).T

    total = cross_out[s]
    for j in range(1, ns):
        q = sample_peer(ns - j)
        copy(cross_out.at[q], cross_in.at[q], cross_send.at[j], cross_recv.at[j], q, v).wait_recv()
        total = total + cross_in[q]
    cross_sum[s] = total[:, :piece]

    def sum_copy(j, slot, p):
        return copy(cross_sum.at[s], cross_sum.at[slot], sum_send.at[j], sum_recv.at[j], p, v)

    for j in range(1, ns):
        start(sum_copy(j, s, sample_peer(j)))
    packed = total[:, piece:]
    shares = [packed[:, r * depth : (r + 1) * depth] for r in range(depth // ROWS)]
    moment = jnp.concatenate(shares, 0)
    row_at = lax.broadcasted_iota(jnp.int32, moment.shape, 0)
    lane_at = lax.broadcasted_iota(jnp.int32, moment.shape, 1)
    moment = jnp.where((row_at == lane_at) & (row_at >= terms), 1.0, moment)
    solve = eliminate(moment, 0, depth)
    block_copy(1, 0).wait_recv()
    start(block_copy(2, 0))
    for j in range(1, ns):
        q = sample_peer(ns - j)
        sum_copy(j, q, q).wait_recv()
    for i in range(ns):
        r, c = divmod(i, across)
        cross[r * ROWS : (r + 1) * ROWS, c * piece : (c + 1) * piece] = cross_sum[i]
    coefs[0] = exact_dot(solve, cross[...], contract)

    def coef_copy(k):
        return copy(coefs.at[0], coefs.at[k], coef_send.at[k], coef_recv.at[k], s, variant_peer(-k))

    for k in (1, 2):
        start(coef_copy(k))
    block_copy(1, 1).wait_recv()
    start(block_copy(2, 1))

    mine = own_t[...] - fast_dot(right_terms(coefs[0], 0), terms_ref[...], ((0,), (0,)))
    own_b[...] = mine.astype(BF16)
    own_t[...] = mine
    partner = group * 2 + 1 - half
    order = list(range(1, groups)) + [0]

    def store_spread(k, values):
        spreads[s, k : k + 1] = values[:, : width // 2]
        spreads[s, k + 3 : k + 4] = values[:, width // 2 :]

    def residual(k):
        coef_copy(k).wait_recv()
        if k == 2:
            for part in (0, 1):
                block_copy(2, part).wait_recv()
        fitted = fast_dot(terms_ref[...], right_terms(coefs[k], 0), ((0,), (0,)))
        theirs = blocks[k - 1].astype(F32) - fitted
        tiles[k - 1] = fast_dot(own_b[...], theirs.astype(BF16), contract)
        store_spread(k, jnp.sum(theirs * theirs, 0, keepdims=True))

    def slot(k, j):
        return (k - 1) * groups + j

    def pair_copy(k, j):
        i = slot(k, j)
        return copy(pair_out.at[i], pair_in.at[i], pair_send.at[i], pair_recv.at[i], partner, v)

    def ring_copy(k, j):
        i = slot(k, j)
        target = lax.rem(group + j, groups) * 2 + half
        return copy(ring_out.at[i], ring_in.at[i], ring_send.at[i], ring_recv.at[i], target, v)

    def give(k, j):
        i = slot(k, j)
        g = lax.rem(group + j, groups)
        at = pl.multiple_of((g * 2 + 1 - half) * rows, rows)
        pair_out[i] = tiles[k - 1, pl.ds(at, rows)].astype(BF16)
        start(pair_copy(k, j))

    def take(k, j):
        i = slot(k, j)
        pair_copy(k, j).wait_recv()
        g = lax.rem(group + j, groups)
        at = pl.multiple_of((g * 2 + half) * rows, rows)
        summed = tiles[k - 1, pl.ds(at, rows)] + pair_in[i].astype(F32)
        if j:
            ring_out[i] = summed.astype(BF16)
            start(ring_copy(k, j))
        return summed

    def gather(k, summed):
        for j in range(1, groups):
            ring_copy(k, j).wait_recv()
            summed = summed + ring_in[slot(k, j)].astype(F32)
        return summed

    residual(1)
    early_sends = len(sent)
    for j in order:
        give(1, j)
    column = jnp.sum(mine * mine, 1, keepdims=True)
    store_spread(0, jnp.broadcast_to(column, (width, LANES)).T[0:1])
    spreads[s, 6:ROWS] = jnp.zeros((ROWS - 6, width // 2), F32)
    for j in order[:1]:
        take(1, j)
    flush(early_sends)
    residual(2)
    for j in range(1, ns):
        p = sample_peer(j)
        start(copy(spreads.at[s], spreads.at[s], spread_send.at[j], spread_recv.at[j], p, v))
    for n, j in enumerate(order):
        give(2, j)
        if n:
            last = take(1, j)

    middle_sends = len(sent)
    spread = spreads[s]
    for j in range(1, ns):
        q = sample_peer(ns - j)
        copy(spreads.at[q], spreads.at[q], spread_send.at[j], spread_recv.at[j], q, v).wait_recv()
        spread = spread + spreads[q]
    scale = jnp.sqrt(samples / jnp.concatenate([spread[0:3], spread[3:6]], 1))
    chosen = lax.broadcasted_iota(jnp.int32, (rows, width), 1) == (
        lax.broadcasted_iota(jnp.int32, (rows, width), 0) + s * rows
    )
    scale_rows = jnp.sum(jnp.where(chosen, scale[0:1], 0.0), 1, keepdims=True)
    scale_rows = scale_rows * (1.0 / math.sqrt(samples))
    load_reach.wait()
    own_reach = reach[v]

    def masked(k, tile):
        return jnp.where(own_reach >= k, tile.astype(F32), 0.0).astype(BF16)

    def finish(k, summed):
        part = summed * scale_rows * scale[k : k + 1]
        out[MAXR + k - 1] = masked(k, part)
        return part

    def turn_copy(k, j, p, q):
        return copy(turn_out.at[k - 1, p], turn_in.at[k - 1, q], turn_send.at[(k - 1) * ns + j],
                    turn_recv.at[(k - 1) * ns + j], p, v)

    def turn_start(k, part):
        for i in range(ns):
            turn_out[k - 1, i] = part[:, i * rows : (i + 1) * rows].astype(BF16)
        for j in range(1, ns):
            start(turn_copy(k, j, sample_peer(j), s))
        turn_in[k - 1, s] = turn_out[k - 1, s]

    def back_copy(k):
        return copy(back_out.at[k - 1], back_in.at[k - 1], back_send.at[k - 1],
                    back_recv.at[k - 1], s, variant_peer(k))

    def turn_end(k):
        for j in range(1, ns):
            q = sample_peer(ns - j)
            turn_copy(k, j, q, q).wait_recv()
        back_out[k - 1] = turn_in[k - 1].astype(F32).reshape(width, rows).T.astype(BF16)
        start(back_copy(k))

    def back_end(k):
        back_copy(k).wait_recv()
        out[MAXR - k] = masked(k, back_in[k - 1])

    early = len(order) // 2
    for j in order[:early]:
        take(2, j)
    turn_start(1, finish(1, gather(1, last)))
    for j in order[early:]:
        last = take(2, j)
    flush(middle_sends)
    turn_end(1)
    part = finish(2, gather(2, last))
    if 4 % nb:
        turn_start(2, part)
        turn_end(2)
        back_end(2)
    else:
        out[MAXR - 2] = masked(2, part)
    back_end(1)
    flush(len(sent))


def shards(dosage, covariates, reach):
    ns, nb = lax.axis_size("sample"), lax.axis_size("variant")
    local, width = dosage.shape
    depth = -(-(covariates.shape[0] + 1) // 32) * 32
    piece = width * (depth // ROWS) // ns
    groups, rows = ns // 2, width // ns
    vmem = pltpu.VMEM
    pair = lambda n: [pltpu.SemaphoreType.DMA((n,))] * 2
    return pl.pallas_call(
        functools.partial(kernel, ns, nb),
        out_shape=jax.ShapeDtypeStruct((2 * MAXR, rows, width), BF16),
        in_specs=[pl.BlockSpec(memory_space=pltpu.HBM)] * 3,
        out_specs=pl.BlockSpec(memory_space=pltpu.VMEM),
        scratch_shapes=[
            vmem((local, width), BF16),
            vmem(covariates.shape, F32),
            pltpu.SMEM(reach.shape, jnp.int32),
            vmem((LANES, local), F32),
            vmem((6 * depth, local), BF16),
            vmem((depth, width), F32),
            vmem((ns, ROWS, piece + LANES), F32),
            vmem((ns, ROWS, piece + LANES), F32),
            vmem((ns, ROWS, piece), F32),
            vmem((3, depth, width), F32),
            vmem((2, local, width), BF16),
            vmem((width, local), F32),
            vmem((width, local), BF16),
            vmem((ns, ROWS, width // 2), F32),
            vmem((2, width, width), F32),
            vmem((2 * groups, rows, width), BF16),
            vmem((2 * groups, rows, width), BF16),
            vmem((2 * groups, rows, width), BF16),
            vmem((2 * groups, rows, width), BF16),
            vmem((2, ns, rows, rows), BF16),
            vmem((2, ns, rows, rows), BF16),
            vmem((2, rows, width), BF16),
            vmem((2, rows, width), BF16),
            pltpu.SemaphoreType.DMA((3,)),
            *pair(4), *pair(ns), *pair(ns), *pair(3), *pair(ns), *pair(2 * groups),
            *pair(2 * groups), *pair(2 * ns), *pair(2),
        ],
        compiler_params=pltpu.CompilerParams(
            collective_id=0, has_side_effects=True, vmem_limit_bytes=VMEM_LIMIT
        ),
    )(dosage, covariates, reach)


def solution(mesh):
    placed = (P("sample", "variant"), P(None, "sample"), P())
    return jax.shard_map(
        shards,
        mesh=mesh,
        in_specs=placed,
        out_specs=P(None, ("variant", "sample"), None),
        check_vma=False,
    )
```

```python
import functools
import math

import jax
import jax.numpy as jnp
from jax import lax
from jax.experimental import pallas as pl
from jax.experimental.pallas import tpu as pltpu
from jax.sharding import PartitionSpec as P

MAXR = 2
ROWS = 8
LANES = 128
VMEM_LIMIT = 63 * 1024 * 1024
MESH = pl.DeviceIdType.MESH
HIGHEST = lax.Precision.HIGHEST
F32 = jnp.float32
BF16 = jnp.bfloat16


def exact_dot(a, b, dims):
    return lax.dot_general(a, b, (dims, ((), ())), precision=HIGHEST, preferred_element_type=F32)


def pieces(x):
    high = x.astype(BF16)
    left = x - high.astype(F32)
    middle = left.astype(BF16)
    return high, middle, (left - middle.astype(F32)).astype(BF16)


def left_terms(x, axis):
    h, m, l = pieces(x)
    return jnp.concatenate([h, h, m, h, m, l], axis)


def right_terms(x, axis):
    h, m, l = pieces(x)
    return jnp.concatenate([h, m, h, l, m, h], axis)


def fast_dot(a, b, dims):
    return lax.dot_general(a, b, (dims, ((), ())), preferred_element_type=F32)


def eliminate(matrix, first, last):
    row_at = lax.broadcasted_iota(jnp.int32, matrix.shape, 0)
    lane_at = lax.broadcasted_iota(jnp.int32, matrix.shape, 1)
    lane = lane_at[:1]
    for k in range(first, last, 2):
        one = jnp.broadcast_to(matrix[:, k : k + 1], matrix.shape)
        two = jnp.broadcast_to(matrix[:, k + 1 : k + 2], matrix.shape)
        a, c = one[k : k + 1], one[k + 1 : k + 2]
        b, d = two[k : k + 1], two[k + 1 : k + 2]
        upper = jnp.where(lane == k, 1.0, jnp.where(lane == k + 1, 0.0, matrix[k : k + 1]))
        lower = jnp.where(lane == k, 0.0, jnp.where(lane == k + 1, 1.0, matrix[k + 1 : k + 2]))
        ratio = c / a
        lower = (lower - ratio * upper) / (d - ratio * b)
        upper = (upper - b * lower) / a
        rest = jnp.where((lane_at == k) | (lane_at == k + 1), 0.0, matrix)
        rest = rest - one * upper - two * lower
        matrix = jnp.where(row_at == k, upper, jnp.where(row_at == k + 1, lower, rest))
    return matrix


def kernel(
    ns, nb, dosage_in, covariates_in, reach_in, out,
    dosage, covariates, reach, design, terms_ref, cross, cross_out, cross_in, cross_sum, coefs,
    blocks, own_t, own_b, spreads, tiles, pair_out, pair_in, ring_out, ring_in,
    turn_out, turn_in, back_out, back_in, load_sem,
    block_send, block_recv, cross_send, cross_recv, sum_send, sum_recv, coef_send, coef_recv,
    spread_send, spread_recv, pair_send, pair_recv, ring_send, ring_recv,
    turn_send, turn_recv, back_send, back_recv,
):
    s = lax.axis_index("sample")
    v = lax.axis_index("variant")
    local, width = dosage.shape
    terms = covariates.shape[0] + 1
    depth = cross.shape[0]
    across = ns // (depth // ROWS)
    piece = width // across
    groups = ns // 2
    group, half = lax.div(s, 2), lax.rem(s, 2)
    rows = width // ns
    samples = float(local * ns)

    def sample_peer(j):
        return lax.rem(s + j, ns)

    def variant_peer(j):
        return lax.rem(v + j + nb, nb)

    def copy(src, dst, send, recv, sample, variant):
        return pltpu.make_async_remote_copy(
            src_ref=src, dst_ref=dst, send_sem=send, recv_sem=recv,
            device_id=(sample, variant), device_id_type=MESH,
        )

    load_dosage = pltpu.make_async_copy(dosage_in, dosage, load_sem.at[0])
    load_covariates = pltpu.make_async_copy(covariates_in, covariates, load_sem.at[1])
    load_reach = pltpu.make_async_copy(reach_in, reach, load_sem.at[2])
    load_covariates.start()
    load_dosage.start()
    load_reach.start()

    barrier = pltpu.get_barrier_semaphore()
    hops = sorted({1, 2, nb - 1, nb - 2})
    for j in range(1, ns):
        pl.semaphore_signal(barrier, inc=1, device_id=(sample_peer(j), v), device_id_type=MESH)
    for j in hops:
        pl.semaphore_signal(barrier, inc=1, device_id=(s, variant_peer(j)), device_id_type=MESH)

    sent = []

    def flush(count):
        for c in sent[:count]:
            c.wait_send()
        del sent[:count]

    def start(c):
        c.start()
        sent.append(c)

    contract = ((1,), (0,))
    design[...] = jnp.zeros_like(design)
    design[0:1] = jnp.ones((1, local), F32)
    load_covariates.wait()
    design[1:terms] = covariates[...]
    full = design[0:depth]
    high, middle, low = pieces(full)
    moment = exact_dot(full, design[...], ((1,), (1,)))[:, :depth]
    packed = jnp.concatenate([moment[r : r + ROWS] for r in range(0, depth, ROWS)], 1)
    load_dosage.wait()
    genotype = dosage[...]
    partial = fast_dot(jnp.concatenate([high, middle, low], 0), genotype, contract)
    partial = partial[:depth] + (partial[depth : 2 * depth] + partial[2 * depth :])
    for i in range(ns):
        r, c = divmod(i, across)
        cross_out[i, :, :piece] = partial[r * ROWS : (r + 1) * ROWS, c * piece : (c + 1) * piece]
        cross_out[i, :, piece:] = packed

    pl.semaphore_wait(barrier, ns - 1 + len(hops))
    behind = variant_peer(-1)
    for j in range(1, ns):
        p = sample_peer(j)
        start(copy(cross_out.at[p], cross_in.at[s], cross_send.at[j], cross_recv.at[j], p, v))

    def block_copy(k, part):
        at = pl.ds(part * (local // 2), local // 2)
        src = dosage if k == 1 else blocks.at[0]
        i = (k - 1) * 2 + part
        return copy(src.at[at], blocks.at[k - 1, at], block_send.at[i], block_recv.at[i], s, behind)

    for part in (0, 1):
        start(block_copy(1, part))
    terms_ref[...] = left_terms(full, 0)
    own_t[...] = genotype.astype(F32).T

    total = cross_out[s]
    for j in range(1, ns):
        q = sample_peer(ns - j)
        copy(cross_out.at[q], cross_in.at[q], cross_send.at[j], cross_recv.at[j], q, v).wait_recv()
        total = total + cross_in[q]
    cross_sum[s] = total[:, :piece]

    def sum_copy(j, slot, p):
        return copy(cross_sum.at[s], cross_sum.at[slot], sum_send.at[j], sum_recv.at[j], p, v)

    for j in range(1, ns):
        start(sum_copy(j, s, sample_peer(j)))
    packed = total[:, piece:]
    shares = [packed[:, r * depth : (r + 1) * depth] for r in range(depth // ROWS)]
    moment = jnp.concatenate(shares, 0)
    row_at = lax.broadcasted_iota(jnp.int32, moment.shape, 0)
    lane_at = lax.broadcasted_iota(jnp.int32, moment.shape, 1)
    moment = jnp.where((row_at == lane_at) & (row_at >= terms), 1.0, moment)
    solve = eliminate(moment, 0, depth)
    block_copy(1, 0).wait_recv()
    start(block_copy(2, 0))
    for j in range(1, ns):
        q = sample_peer(ns - j)
        sum_copy(j, q, q).wait_recv()
    for i in range(ns):
        r, c = divmod(i, across)
        cross[r * ROWS : (r + 1) * ROWS, c * piece : (c + 1) * piece] = cross_sum[i]
    coefs[0] = fast_dot(left_terms(solve, 1), right_terms(cross[...], 0), contract)

    def coef_copy(k):
        return copy(coefs.at[0], coefs.at[k], coef_send.at[k], coef_recv.at[k], s, variant_peer(-k))

    for k in (1, 2):
        start(coef_copy(k))
    block_copy(1, 1).wait_recv()
    start(block_copy(2, 1))

    mine = own_t[...] - fast_dot(right_terms(coefs[0], 0), terms_ref[...], ((0,), (0,)))
    own_b[...] = mine.astype(BF16)
    own_t[...] = mine
    partner = group * 2 + 1 - half
    order = list(range(1, groups)) + [0]

    def store_spread(k, values):
        spreads[s, k : k + 1] = values[:, : width // 2]
        spreads[s, k + 3 : k + 4] = values[:, width // 2 :]

    def residual(k):
        coef_copy(k).wait_recv()
        if k == 2:
            for part in (0, 1):
                block_copy(2, part).wait_recv()
        fitted = fast_dot(terms_ref[...], right_terms(coefs[k], 0), ((0,), (0,)))
        theirs = blocks[k - 1].astype(F32) - fitted
        tiles[k - 1] = fast_dot(own_b[...], theirs.astype(BF16), contract)
        store_spread(k, jnp.sum(theirs * theirs, 0, keepdims=True))

    def slot(k, j):
        return (k - 1) * groups + j

    def pair_copy(k, j):
        i = slot(k, j)
        return copy(pair_out.at[i], pair_in.at[i], pair_send.at[i], pair_recv.at[i], partner, v)

    def ring_copy(k, j):
        i = slot(k, j)
        target = lax.rem(group + j, groups) * 2 + half
        return copy(ring_out.at[i], ring_in.at[i], ring_send.at[i], ring_recv.at[i], target, v)

    def give(k, j):
        i = slot(k, j)
        g = lax.rem(group + j, groups)
        at = pl.multiple_of((g * 2 + 1 - half) * rows, rows)
        pair_out[i] = tiles[k - 1, pl.ds(at, rows)].astype(BF16)
        start(pair_copy(k, j))

    def take(k, j):
        i = slot(k, j)
        pair_copy(k, j).wait_recv()
        g = lax.rem(group + j, groups)
        at = pl.multiple_of((g * 2 + half) * rows, rows)
        summed = tiles[k - 1, pl.ds(at, rows)] + pair_in[i].astype(F32)
        if j:
            ring_out[i] = summed.astype(BF16)
            start(ring_copy(k, j))
        return summed

    def gather(k, summed):
        for j in range(1, groups):
            ring_copy(k, j).wait_recv()
            summed = summed + ring_in[slot(k, j)].astype(F32)
        return summed

    residual(1)
    early_sends = len(sent)
    for j in order:
        give(1, j)
    column = jnp.sum(mine * mine, 1, keepdims=True)
    store_spread(0, jnp.broadcast_to(column, (width, LANES)).T[0:1])
    spreads[s, 6:ROWS] = jnp.zeros((ROWS - 6, width // 2), F32)
    for j in order[:1]:
        take(1, j)
    flush(early_sends)
    residual(2)
    for j in range(1, ns):
        p = sample_peer(j)
        start(copy(spreads.at[s], spreads.at[s], spread_send.at[j], spread_recv.at[j], p, v))
    for n, j in enumerate(order):
        give(2, j)
        if n:
            last = take(1, j)

    middle_sends = len(sent)
    spread = spreads[s]
    for j in range(1, ns):
        q = sample_peer(ns - j)
        copy(spreads.at[q], spreads.at[q], spread_send.at[j], spread_recv.at[j], q, v).wait_recv()
        spread = spread + spreads[q]
    scale = jnp.sqrt(samples / jnp.concatenate([spread[0:3], spread[3:6]], 1))
    chosen = lax.broadcasted_iota(jnp.int32, (rows, width), 1) == (
        lax.broadcasted_iota(jnp.int32, (rows, width), 0) + s * rows
    )
    scale_rows = jnp.sum(jnp.where(chosen, scale[0:1], 0.0), 1, keepdims=True)
    scale_rows = scale_rows * (1.0 / math.sqrt(samples))
    load_reach.wait()
    own_reach = reach[v]

    def masked(k, tile):
        return jnp.where(own_reach >= k, tile.astype(F32), 0.0).astype(BF16)

    def finish(k, summed):
        part = summed * scale_rows * scale[k : k + 1]
        out[MAXR + k - 1] = masked(k, part)
        return part

    def turn_copy(k, j, p, q):
        return copy(turn_out.at[k - 1, p], turn_in.at[k - 1, q], turn_send.at[(k - 1) * ns + j],
                    turn_recv.at[(k - 1) * ns + j], p, v)

    def turn_start(k, part):
        for i in range(ns):
            turn_out[k - 1, i] = part[:, i * rows : (i + 1) * rows].astype(BF16)
        for j in range(1, ns):
            start(turn_copy(k, j, sample_peer(j), s))
        turn_in[k - 1, s] = turn_out[k - 1, s]

    def back_copy(k):
        return copy(back_out.at[k - 1], back_in.at[k - 1], back_send.at[k - 1],
                    back_recv.at[k - 1], s, variant_peer(k))

    def turn_end(k):
        for j in range(1, ns):
            q = sample_peer(ns - j)
            turn_copy(k, j, q, q).wait_recv()
        back_out[k - 1] = turn_in[k - 1].astype(F32).reshape(width, rows).T.astype(BF16)
        start(back_copy(k))

    def back_end(k):
        back_copy(k).wait_recv()
        out[MAXR - k] = masked(k, back_in[k - 1])

    early = len(order) // 2
    for j in order[:early]:
        take(2, j)
    turn_start(1, finish(1, gather(1, last)))
    for j in order[early:]:
        last = take(2, j)
    flush(middle_sends)
    turn_end(1)
    part = finish(2, gather(2, last))
    if 4 % nb:
        turn_start(2, part)
        turn_end(2)
        back_end(2)
    else:
        out[MAXR - 2] = masked(2, part)
    back_end(1)
    flush(len(sent))


def shards(dosage, covariates, reach):
    ns, nb = lax.axis_size("sample"), lax.axis_size("variant")
    local, width = dosage.shape
    depth = -(-(covariates.shape[0] + 1) // 32) * 32
    piece = width * (depth // ROWS) // ns
    groups, rows = ns // 2, width // ns
    vmem = pltpu.VMEM
    pair = lambda n: [pltpu.SemaphoreType.DMA((n,))] * 2
    return pl.pallas_call(
        functools.partial(kernel, ns, nb),
        out_shape=jax.ShapeDtypeStruct((2 * MAXR, rows, width), BF16),
        in_specs=[pl.BlockSpec(memory_space=pltpu.HBM)] * 3,
        out_specs=pl.BlockSpec(memory_space=pltpu.VMEM),
        scratch_shapes=[
            vmem((local, width), BF16),
            vmem(covariates.shape, F32),
            pltpu.SMEM(reach.shape, jnp.int32),
            vmem((LANES, local), F32),
            vmem((6 * depth, local), BF16),
            vmem((depth, width), F32),
            vmem((ns, ROWS, piece + LANES), F32),
            vmem((ns, ROWS, piece + LANES), F32),
            vmem((ns, ROWS, piece), F32),
            vmem((3, depth, width), F32),
            vmem((2, local, width), BF16),
            vmem((width, local), F32),
            vmem((width, local), BF16),
            vmem((ns, ROWS, width // 2), F32),
            vmem((2, width, width), F32),
            vmem((2 * groups, rows, width), BF16),
            vmem((2 * groups, rows, width), BF16),
            vmem((2 * groups, rows, width), BF16),
            vmem((2 * groups, rows, width), BF16),
            vmem((2, ns, rows, rows), BF16),
            vmem((2, ns, rows, rows), BF16),
            vmem((2, rows, width), BF16),
            vmem((2, rows, width), BF16),
            pltpu.SemaphoreType.DMA((3,)),
            *pair(4), *pair(ns), *pair(ns), *pair(3), *pair(ns), *pair(2 * groups),
            *pair(2 * groups), *pair(2 * ns), *pair(2),
        ],
        compiler_params=pltpu.CompilerParams(
            collective_id=0, has_side_effects=True, vmem_limit_bytes=VMEM_LIMIT
        ),
    )(dosage, covariates, reach)


def solution(mesh):
    placed = (P("sample", "variant"), P(None, "sample"), P())
    return jax.shard_map(
        shards,
        mesh=mesh,
        in_specs=placed,
        out_specs=P(None, ("variant", "sample"), None),
        check_vma=False,
    )
```
